32 devices in a mesh: path: 8 (over z, x), fsdp: 4 (over y, core).
Axes of the slice: x: 2, y: 2, z: 4, core: 2. Of those that a mesh axis runs over, the one named last changes fastest.
Arguments:
- hidden_in: bfloat16 [8, 512, 1024], P('path', 'fsdp'), may hold values from -40 to 40
- cotangent: bfloat16 [8, 512, 1024], P('path', 'fsdp'), may hold values from -6 to 6
- up_weight: bfloat16 [8, 1024, 4096], P(None, 'path', 'fsdp'), may hold values from -4 to 4
- down_weight: bfloat16 [8, 1024, 4096], P(None, 'path', 'fsdp'), may hold values from -4 to 4
- up_moment: bfloat16 [8, 1024, 4096], P(None, 'path', 'fsdp'), may hold values from -3 to 3
- down_moment: bfloat16 [8, 1024, 4096], P(None, 'path', 'fsdp'), may hold values from -3 to 3
- sharing: int32 [8, 2], replicated, may hold values from 0 to 7, as said below
Outputs:
- new_up: bfloat16 [8, 1024, 4096], P(None, 'path', 'fsdp')
- new_down: bfloat16 [8, 1024, 4096], P(None, 'path', 'fsdp')
- new_up_moment: bfloat16 [8, 1024, 4096], P(None, 'path', 'fsdp')
- new_down_moment: bfloat16 [8, 1024, 4096], P(None, 'path', 'fsdp')
The draws below stay inside these ranges and needn't reach their ends.
Inputs may be any that keep to these rules, and one draw needn't show every extreme that they name: `sharing`: column 0 names a first-level module, 0 to 3; column 1 a second-level module, 4 to 7. Every module is named by at least one path.
All inputs are finite; a program needn't handle non-finite values.
Results may differ from the reference program's by a relative error of at most 0.014.
Values may be sent and summed in bfloat16 or wider, within the bound.
A program may use at most 128 MiB of HBM per device.

```python
import math
import jax
import jax.numpy as jnp
from jax import lax

D = 1024
HID = 4096
PATHS = 8
MODS = 4
NMOD = 8
PATH_TOK = 512


def draw_hidden_in(key, part):
    key = jax.random.fold_in(key, 11)
    key_base, key_rows, key_cols = jax.random.split(key, 3)
    base = jax.random.truncated_normal(key_base, -4.0, 4.0, (PATHS, PATH_TOK, D), jnp.float32)
    spread = 1.15
    row_factor = jnp.exp(jax.random.uniform(key_rows, (PATHS, PATH_TOK, 1), jnp.float32, -spread, spread))
    col_factor = jnp.exp(jax.random.uniform(key_cols, (1, 1, D), jnp.float32, -spread, spread))
    return (base * row_factor * col_factor).astype(jnp.bfloat16)


def level_column(key, level):
    key = jax.random.fold_in(key, level)
    key_one, key_two, key_three, key_label, key_order = jax.random.split(key, 5)
    extra = jnp.minimum(jax.random.randint(key_one, (PATHS - MODS,), 0, MODS), jax.random.randint(key_two, (PATHS - MODS,), 0, MODS))
    extra = jnp.minimum(extra, jax.random.randint(key_three, (PATHS - MODS,), 0, MODS))
    labels = jnp.concatenate([jnp.arange(MODS, dtype=jnp.int32), extra.astype(jnp.int32)])
    relabel = jax.random.permutation(key_label, MODS).astype(jnp.int32)
    order = jax.random.permutation(key_order, PATHS)
    return relabel[labels][order] + level * MODS


def draw_sharing(key, part):
    key = jax.random.fold_in(key, 7)
    return jnp.stack([level_column(key, 0), level_column(key, 1)], axis=1).astype(jnp.int32)


def block_levels(rng, extent, cuts, smallest, largest):
    level = 1.0
    for axis_at, parts in cuts:
        steps = jax.random.uniform(jax.random.fold_in(jax.random.fold_in(rng, 6), axis_at), (parts,), jnp.float32, smallest / len(cuts), largest / len(cuts))
        level = level * jnp.repeat(jnp.exp(steps), extent[axis_at] // parts).reshape((-1,) + (1,) * (len(extent) - 1 - axis_at))
    return level


def noise(stream_key, extent, width, most, pieces=(), kind=jnp.bfloat16):
    result = width * jax.random.normal(stream_key, extent, jnp.float32)
    if pieces:
        result = result * block_levels(stream_key, extent, pieces, -0.22, 0.18)
    return jnp.clip(result, -most, most).astype(kind)


def setup_inputs(seed: int = 0) -> dict:
    key_of = jax.random.split(jax.random.key(seed), 8)
    hidden_in = draw_hidden_in(jax.random.fold_in(key_of[7], 71), 0)
    cotangent = noise(key_of[1], (PATHS, PATH_TOK, D), 1.0, 6.0, ((0, 8), (1, 4)))
    up_weight = noise(key_of[2], (NMOD, D, HID), 1.0, 4.0, ((1, 8), (2, 4)))
    down_weight = noise(key_of[3], (NMOD, D, HID), 1.0, 4.0, ((1, 8), (2, 4)))
    up_moment = noise(key_of[4], (NMOD, D, HID), 0.5, 3.0, ((1, 8), (2, 4)))
    down_moment = noise(key_of[5], (NMOD, D, HID), 0.5, 3.0, ((1, 8), (2, 4)))
    sharing = draw_sharing(jax.random.fold_in(key_of[7], 71), 0)
    return {"hidden_in": hidden_in, "cotangent": cotangent, "up_weight": up_weight, "down_weight": down_weight, "up_moment": up_moment, "down_moment": down_moment, "sharing": sharing}


inner_rate = 2.0
outer_rate = 0.7
keep_rate = 0.9
norm_eps = 1e-06
tanh_coeff = 0.7978845608028654
cube_coeff = 0.044715

def gelu_value(values):
    inside = tanh_coeff * (values + cube_coeff * values * values * values)
    return 0.5 * values * (1.0 + jnp.tanh(inside))

def gelu_slope(values):
    inside = tanh_coeff * (values + cube_coeff * values * values * values)
    tangent = jnp.tanh(inside)
    return 0.5 * (1.0 + tangent) + 0.5 * values * (1.0 - tangent * tangent) * tanh_coeff * (1.0 + 3.0 * cube_coeff * values * values)

def row_scale(values):
    return lax.rsqrt(lax.optimization_barrier(jnp.mean(values * values, axis=-1, keepdims=True)) + norm_eps)

def path_deltas(tokens_in, cot_in, up_first, down_first, up_second, down_second):
    in_scale = 1.0 / math.sqrt(up_first.shape[0])
    hid_scale = 1.0 / math.sqrt(up_first.shape[1])
    start_vals = tokens_in.astype(jnp.float32)
    normed_first = (start_vals * row_scale(start_vals)).astype(jnp.bfloat16)
    pre_first = jnp.dot(normed_first, up_first, preferred_element_type=jnp.float32) * in_scale
    hidden_first = gelu_value(pre_first).astype(jnp.bfloat16)
    middle = start_vals + jnp.dot(hidden_first, down_first.T, preferred_element_type=jnp.float32) * hid_scale
    scale_second = row_scale(middle)
    unit_second = middle * scale_second
    normed_second = unit_second.astype(jnp.bfloat16)
    pre_second = jnp.dot(normed_second, up_second, preferred_element_type=jnp.float32) * in_scale
    hidden_second = gelu_value(pre_second).astype(jnp.bfloat16)
    back_hidden = jnp.dot(cot_in, down_second, preferred_element_type=jnp.float32) * hid_scale
    grad_down_second = jnp.dot(cot_in.T, hidden_second, preferred_element_type=jnp.float32) * hid_scale
    back_pre = (back_hidden * gelu_slope(pre_second)).astype(jnp.bfloat16)
    grad_up_second = jnp.dot(normed_second.T, back_pre, preferred_element_type=jnp.float32) * in_scale
    back_normed = jnp.dot(back_pre, up_second.T, preferred_element_type=jnp.float32) * in_scale
    back_middle = (cot_in.astype(jnp.float32) + scale_second * (back_normed - unit_second * lax.optimization_barrier(jnp.mean(back_normed * unit_second, axis=-1, keepdims=True)))).astype(jnp.bfloat16)
    back_hidden_first = jnp.dot(back_middle, down_first, preferred_element_type=jnp.float32) * hid_scale
    grad_down_first = jnp.dot(back_middle.T, hidden_first, preferred_element_type=jnp.float32) * hid_scale
    back_pre_first = (back_hidden_first * gelu_slope(pre_first)).astype(jnp.bfloat16)
    grad_up_first = jnp.dot(normed_first.T, back_pre_first, preferred_element_type=jnp.float32) * in_scale
    delta_up = (inner_rate * jnp.stack([grad_up_first, grad_up_second])).astype(jnp.bfloat16)
    delta_down = (inner_rate * jnp.stack([grad_down_first, grad_down_second])).astype(jnp.bfloat16)
    return (delta_up, delta_down)

def outer_step(weight, moment, mean_delta):
    new_moment = keep_rate * moment.astype(jnp.float32) + mean_delta
    new_weight = weight.astype(jnp.float32) - outer_rate * (mean_delta + keep_rate * new_moment)
    return (new_weight.astype(jnp.bfloat16), new_moment.astype(jnp.bfloat16))

def reference(hidden_in, cotangent, up_weight, down_weight, up_moment, down_moment, sharing):
    module_count = up_weight.shape[0]

    def one_path(totals, inputs):
        tokens_in, cot_in, pair = inputs
        first = pair[0].astype(jnp.int32)
        second = pair[1].astype(jnp.int32)
        up_first = lax.dynamic_index_in_dim(up_weight, first, 0, keepdims=False)
        down_first = lax.dynamic_index_in_dim(down_weight, first, 0, keepdims=False)
        up_second = lax.dynamic_index_in_dim(up_weight, second, 0, keepdims=False)
        down_second = lax.dynamic_index_in_dim(down_weight, second, 0, keepdims=False)
        delta_up, delta_down = path_deltas(tokens_in, cot_in, up_first, down_first, up_second, down_second)
        total_up, total_down = totals
        total_up = total_up.at[first].add(delta_up[0].astype(jnp.float32)).at[second].add(delta_up[1].astype(jnp.float32))
        total_down = total_down.at[first].add(delta_down[0].astype(jnp.float32)).at[second].add(delta_down[1].astype(jnp.float32))
        return ((total_up, total_down), None)
    zeros = jnp.zeros(up_weight.shape, jnp.float32)
    totals, unused_out = lax.scan(one_path, (zeros, zeros), (hidden_in, cotangent, sharing))
    total_up, total_down = totals
    hits = (sharing[:, :, None] == jnp.arange(module_count, dtype=jnp.int32)[None, None, :]).astype(jnp.float32)
    counts = lax.optimization_barrier(jnp.sum(hits, axis=(0, 1)))
    mean_up = total_up / counts[:, None, None]
    mean_down = total_down / counts[:, None, None]
    new_up, new_up_moment = outer_step(up_weight, up_moment, mean_up)
    new_down, new_down_moment = outer_step(down_weight, down_moment, mean_down)
    return (new_up, new_down, new_up_moment, new_down_moment)
```

```python
import functools
import math

import jax
import jax.numpy as jnp
from jax import lax
from jax.experimental import pallas as pl
from jax.experimental.pallas import tpu as pltpu
from jax.sharding import PartitionSpec as P

inner_rate = 2.0
outer_rate = 0.7
keep_rate = 0.9
norm_eps = 1e-06
tanh_coeff = 0.7978845608028654
cube_coeff = 0.044715
MESH = pl.DeviceIdType.MESH


def gelu_both(values):
    inside = tanh_coeff * (values + cube_coeff * values * values * values)
    tangent = jnp.tanh(inside)
    value = 0.5 * values * (1.0 + tangent)
    slope = 0.5 * (1.0 + tangent) + 0.5 * values * (1.0 - tangent * tangent) * tanh_coeff * (
        1.0 + 3.0 * cube_coeff * values * values
    )
    return value, slope


def row_scale(values):
    return lax.rsqrt(jnp.mean(values * values, axis=-1, keepdims=True) + norm_eps)


def dot(left, right, dims=((1,), (0,))):
    return lax.dot_general(left, right, (dims, ((), ())), preferred_element_type=jnp.float32)


def each(count, act):
    def step(j, carry):
        act(j)
        return carry

    lax.fori_loop(1, count, step, 0)


def tiles(total, size, act):
    def step(j, carry):
        act(pl.ds(pl.multiple_of(j * size, size), size))
        return carry

    lax.fori_loop(0, total // size, step, 0)


def window_kernel(
    paths, shards, x_ref, g_ref, send_up, send_down, came,
    wbuf, gbuf, norm1, norm2, cot, backmid, hid1, hid2, backpre, slope1, slope2,
    part, sums, middle,
    w_send, w_recv, g_send, g_recv, a_send, a_recv, r_send, r_recv, local_w, local_g,
):
    me = lax.axis_index("path")
    mine = lax.axis_index("fsdp")
    piece, cols = send_up.shape[1:]
    rows, depth = x_ref.shape
    in_scale = 1.0 / math.sqrt(depth)
    hid_scale = 1.0 / math.sqrt(cols * shards)
    tile = 256

    def block(at, size):
        return pl.ds(pl.multiple_of(at * size, size), size)

    def weight_copy(k, j, to):
        source = (send_up, send_down)[k % 2]
        return pltpu.make_async_remote_copy(
            src_ref=source.at[(k // 2) * paths + to],
            dst_ref=wbuf.at[k, block(me, piece)],
            send_sem=w_send.at[k, j], recv_sem=w_recv.at[k, j],
            device_id=(to, mine), device_id_type=MESH,
        )

    def weight_start(k):
        each(paths, lambda j: weight_copy(k, j, lax.rem(me + j, paths)).start())

    def weight_own(k):
        source = (send_up, send_down)[k % 2]
        return pltpu.make_async_copy(
            source.at[(k // 2) * paths + me], wbuf.at[k, block(me, piece)], local_w.at[k]
        )

    def weight_wait(k):
        def act(j):
            origin = lax.rem(me + paths - j, paths)
            pltpu.make_async_remote_copy(
                src_ref=wbuf.at[k, block(origin, piece)],
                dst_ref=wbuf.at[k, block(origin, piece)],
                send_sem=w_send.at[k, j], recv_sem=w_recv.at[k, j],
                device_id=(origin, mine), device_id_type=MESH,
            ).wait_recv()

        each(paths, act)
        weight_own(k).wait()

    def grad_copy(k, j, to):
        return pltpu.make_async_remote_copy(
            src_ref=gbuf.at[k, block(to, piece)],
            dst_ref=came.at[k, me],
            send_sem=g_send.at[k, j], recv_sem=g_recv.at[k, j],
            device_id=(to, mine), device_id_type=MESH,
        )

    def grad_own(k):
        return pltpu.make_async_copy(gbuf.at[k, block(me, piece)], came.at[k, me], local_g.at[k])

    def grad_start(k):
        each(paths, lambda j: grad_copy(k, j, lax.rem(me + j, paths)).start())
        grad_own(k).start()

    def grad_wait(k):
        def act(j):
            origin = lax.rem(me + paths - j, paths)
            pltpu.make_async_remote_copy(
                src_ref=came.at[k, origin], dst_ref=came.at[k, origin],
                send_sem=g_send.at[k, j], recv_sem=g_recv.at[k, j],
                device_id=(origin, mine), device_id_type=MESH,
            ).wait_recv()

        each(paths, act)
        grad_own(k).wait()

    def rows_copy(i, buf, at, j, to):
        return pltpu.make_async_remote_copy(
            src_ref=buf.at[block(at, rows)], dst_ref=buf.at[block(at, rows)],
            send_sem=a_send.at[i, j], recv_sem=a_recv.at[i, j],
            device_id=(me, to), device_id_type=MESH,
        )

    def rows_start(i, buf):
        each(shards, lambda j: rows_copy(i, buf, mine, j, lax.rem(mine + j, shards)).start())

    def rows_wait(i, buf):
        def act(j):
            origin = lax.rem(mine + shards - j, shards)
            rows_copy(i, buf, origin, j, origin).wait_recv()

        each(shards, act)

    def sum_copy(i, j, to):
        return pltpu.make_async_remote_copy(
            src_ref=part.at[i, to], dst_ref=sums.at[i, j],
            send_sem=r_send.at[i, j], recv_sem=r_recv.at[i, j],
            device_id=(me, to), device_id_type=MESH,
        )

    def sum_parts(i, left, k, factor):
        def product(to):
            part[i, to] = dot(left[block(to, rows), :], wbuf[k], ((1,), (1,))) * factor

        def act(j):
            to = lax.rem(mine + j, shards)
            product(to)
            sum_copy(i, j, to).start()

        each(shards, act)
        product(mine)

    def sum_wait(i):
        each(shards, lambda j: sum_copy(i, j, lax.rem(mine + j, shards)).wait_recv())
        total = part[i, mine]
        for j in range(1, shards):
            total = total + sums[i, j]
        return total

    def grad_product(k, left, right, factor):
        def act(at):
            gbuf[k, :, at] = (
                inner_rate * (dot(left[...], right[:, at], ((0,), (0,))) * factor)
            ).astype(jnp.bfloat16)

        tiles(cols, tile, act)
        grad_start(k)

    barrier = pltpu.get_barrier_semaphore()
    each(paths, lambda j: pl.semaphore_signal(
        barrier, inc=1, device_id=(lax.rem(me + j, paths), mine), device_id_type=MESH))
    each(shards, lambda j: pl.semaphore_signal(
        barrier, inc=1, device_id=(me, lax.rem(mine + j, shards)), device_id_type=MESH))
    pl.semaphore_wait(barrier, paths + shards - 2)

    weight_start(0)
    weight_start(1)
    for k in range(4):
        weight_own(k).start()
    tokens = x_ref[...].astype(jnp.float32)
    norm1[block(mine, rows), :] = (tokens * row_scale(tokens)).astype(jnp.bfloat16)
    rows_start(0, norm1)
    cot[block(mine, rows), :] = g_ref[...]
    rows_start(1, cot)
    rows_wait(0, norm1)

    weight_wait(0)
    weight_start(2)

    def forward_first(at):
        value, slope = gelu_both(dot(norm1[...], wbuf[0, :, at]) * in_scale)
        hid1[:, at] = value.astype(jnp.bfloat16)
        slope1[:, at] = slope

    tiles(cols, tile, forward_first)

    weight_wait(1)
    weight_start(3)
    sum_parts(0, hid1, 1, hid_scale)
    mid = x_ref[...].astype(jnp.float32) + sum_wait(0)
    middle[...] = mid
    norm2[block(mine, rows), :] = (mid * row_scale(mid)).astype(jnp.bfloat16)
    rows_start(2, norm2)
    rows_wait(2, norm2)
    rows_wait(1, cot)

    weight_wait(2)

    def forward_second(at):
        value, slope = gelu_both(dot(norm2[...], wbuf[2, :, at]) * in_scale)
        hid2[:, at] = value.astype(jnp.bfloat16)
        slope2[:, at] = slope

    tiles(cols, tile, forward_second)
    grad_product(3, cot, hid2, hid_scale)

    weight_wait(3)

    def back_second(at):
        back = dot(cot[...], wbuf[3, :, at]) * hid_scale
        backpre[1, :, at] = (back * slope2[:, at]).astype(jnp.bfloat16)

    tiles(cols, tile, back_second)
    sum_parts(1, backpre.at[1], 2, in_scale)
    grad_product(2, norm2, backpre.at[1], in_scale)

    back_normed = sum_wait(1)
    mid = middle[...]
    scale = row_scale(mid)
    unit = mid * scale
    centred = back_normed - unit * jnp.mean(back_normed * unit, axis=-1, keepdims=True)
    backmid[block(mine, rows), :] = (
        g_ref[...].astype(jnp.float32) + scale * centred
    ).astype(jnp.bfloat16)
    rows_start(3, backmid)
    rows_wait(3, backmid)
    grad_product(1, backmid, hid1, hid_scale)

    def back_first(at):
        back = dot(backmid[...], wbuf[1, :, at]) * hid_scale
        backpre[0, :, at] = (back * slope1[:, at]).astype(jnp.bfloat16)

    tiles(cols, tile, back_first)
    grad_product(0, norm1, backpre.at[0], in_scale)

    for k in (3, 2, 1, 0):
        grad_wait(k)
    for k in range(4):
        each(paths, lambda j: weight_copy(k, j, lax.rem(me + j, paths)).wait_send())
        each(paths, lambda j: grad_copy(k, j, lax.rem(me + j, paths)).wait_send())
    for i, buf in enumerate((norm1, cot, norm2, backmid)):
        each(shards, lambda j: rows_copy(i, buf, mine, j, lax.rem(mine + j, shards)).wait_send())
    for i in range(2):
        each(shards, lambda j: sum_copy(i, j, lax.rem(mine + j, shards)).wait_send())


def window(paths, shards, tokens, cotangent, send_up, send_down):
    piece, cols = send_up.shape[1:]
    rows, depth = tokens.shape
    total = rows * shards
    bf16, f32 = jnp.bfloat16, jnp.float32
    vmem = pl.BlockSpec(memory_space=pltpu.VMEM)
    anywhere = pl.BlockSpec(memory_space=pl.ANY)
    dma = pltpu.SemaphoreType.DMA
    return pl.pallas_call(
        functools.partial(window_kernel, paths, shards),
        out_shape=jax.ShapeDtypeStruct((4, paths, piece, cols), bf16),
        in_specs=[vmem, vmem, anywhere, anywhere],
        out_specs=anywhere,
        scratch_shapes=[
            pltpu.VMEM((4, depth, cols), bf16),
            pltpu.VMEM((4, depth, cols), bf16),
            pltpu.VMEM((total, depth), bf16),
            pltpu.VMEM((total, depth), bf16),
            pltpu.VMEM((total, depth), bf16),
            pltpu.VMEM((total, depth), bf16),
            pltpu.VMEM((total, cols), bf16),
            pltpu.VMEM((total, cols), bf16),
            pltpu.VMEM((2, total, cols), bf16),
            pltpu.VMEM((total, cols), f32),
            pltpu.VMEM((total, cols), f32),
            pltpu.VMEM((2, shards, rows, depth), f32),
            pltpu.VMEM((2, shards, rows, depth), f32),
            pltpu.VMEM((rows, depth), f32),
            dma((4, paths)), dma((4, paths)),
            dma((4, paths)), dma((4, paths)),
            dma((4, shards)), dma((4, shards)),
            dma((2, shards)), dma((2, shards)),
            dma((4,)), dma((4,)),
        ],
        compiler_params=pltpu.CompilerParams(
            collective_id=0, has_side_effects=True, vmem_limit_bytes=56 * 1024 * 1024
        ),
        cost_estimate=pl.CostEstimate(
            flops=20 * total * depth * cols,
            bytes_accessed=16 * depth * cols * 2,
            transcendentals=2 * total * cols,
        ),
        name="window",
    )(tokens, cotangent, send_up, send_down)


def pick_kernel(chosen, up_ref, down_ref, send_up, send_down):
    send_up[...] = up_ref[...]
    send_down[...] = down_ref[...]


def pick(chosen, up_weight, down_weight):
    modules, piece, cols = up_weight.shape
    count = chosen.shape[0]
    taken = pl.BlockSpec((1, piece, cols), lambda i, ids: (ids[i], 0, 0))
    put = pl.BlockSpec((1, piece, cols), lambda i, ids: (i, 0, 0))
    out = jax.ShapeDtypeStruct((count, piece, cols), jnp.bfloat16)
    return pl.pallas_call(
        pick_kernel,
        out_shape=(out, out),
        grid_spec=pltpu.PrefetchScalarGridSpec(
            num_scalar_prefetch=1, grid=(count,), in_specs=[taken, taken], out_specs=[put, put]
        ),
        name="pick",
    )(chosen, up_weight, down_weight)


def update_kernel(
    paths, half, chosen, came, up, down, up_mom, down_mom,
    new_up, new_down, new_up_mom, new_down_mom, total,
):
    module = pl.program_id(0)
    base = (module // half) * paths

    def tally(q, count):
        return count + (chosen[base + q] == module).astype(jnp.int32)

    count = lax.fori_loop(0, paths, tally, jnp.int32(0)).astype(jnp.float32)
    for k, weight, moment, new_weight, new_moment in (
        (0, up, up_mom, new_up, new_up_mom),
        (1, down, down_mom, new_down, new_down_mom),
    ):
        total[...] = jnp.zeros_like(total)

        def add(q, carry):
            @pl.when(chosen[base + q] == module)
            def _():
                total[...] += came[k, q].astype(jnp.float32)

            return carry

        lax.fori_loop(0, paths, add, 0)
        mean = total[...] / count
        fresh = keep_rate * moment[0].astype(jnp.float32) + mean
        step = weight[0].astype(jnp.float32) - outer_rate * (mean + keep_rate * fresh)
        new_weight[0] = step.astype(jnp.bfloat16)
        new_moment[0] = fresh.astype(jnp.bfloat16)


def update(chosen, came, up, down, up_mom, down_mom):
    modules, piece, cols = up.shape
    paths = came.shape[1]
    half = modules // 2
    one = pl.BlockSpec((1, piece, cols), lambda m, ids: (m, 0, 0))
    level = pl.BlockSpec((2, paths, piece, cols), lambda m, ids: (m // half, 0, 0, 0))
    out = jax.ShapeDtypeStruct(up.shape, jnp.bfloat16)
    return pl.pallas_call(
        functools.partial(update_kernel, paths, half),
        out_shape=(out,) * 4,
        grid_spec=pltpu.PrefetchScalarGridSpec(
            num_scalar_prefetch=1, grid=(modules,), in_specs=[level] + [one] * 4,
            out_specs=[one] * 4, scratch_shapes=[pltpu.VMEM((piece, cols), jnp.float32)],
        ),
        compiler_params=pltpu.CompilerParams(vmem_limit_bytes=48 * 1024 * 1024),
        name="update",
    )(chosen, came, up, down, up_mom, down_mom)


def body(paths, shards, hidden_in, cotangent, up_weight, down_weight, up_moment, down_moment, sharing):
    chosen = jnp.transpose(sharing).reshape(-1)
    send_up, send_down = pick(chosen, up_weight, down_weight)
    came = window(paths, shards, hidden_in[0], cotangent[0], send_up, send_down)
    return update(chosen, came, up_weight, down_weight, up_moment, down_moment)


def solution(mesh):
    weights = P(None, "path", "fsdp")
    tokens = P("path", "fsdp", None)
    return jax.shard_map(
        functools.partial(body, mesh.shape["path"], mesh.shape["fsdp"]),
        mesh=mesh,
        in_specs=(tokens, tokens, weights, weights, weights, weights, P()),
        out_specs=(weights,) * 4,
        check_vma=False,
    )
```

```python
import functools
import math

import jax
import jax.numpy as jnp
from jax import lax
from jax.experimental import pallas as pl
from jax.experimental.pallas import tpu as pltpu
from jax.sharding import PartitionSpec as P

inner_rate = 2.0
outer_rate = 0.7
keep_rate = 0.9
norm_eps = 1e-06
tanh_coeff = 0.7978845608028654
cube_coeff = 0.044715
MESH = pl.DeviceIdType.MESH


def gelu_both(values):
    inside = tanh_coeff * (values + cube_coeff * values * values * values)
    tangent = jnp.tanh(inside)
    value = 0.5 * values * (1.0 + tangent)
    slope = 0.5 * (1.0 + tangent) + 0.5 * values * (1.0 - tangent * tangent) * tanh_coeff * (
        1.0 + 3.0 * cube_coeff * values * values
    )
    return value, slope


def row_scale(values):
    return lax.rsqrt(jnp.mean(values * values, axis=-1, keepdims=True) + norm_eps)


def dot(left, right, dims=((1,), (0,))):
    return lax.dot_general(left, right, (dims, ((), ())), preferred_element_type=jnp.float32)


def loop(first, count, act):
    def step(j, carry):
        act(j)
        return carry

    lax.fori_loop(first, count, step, 0)


def flipped(value, mask):
    bit = 1
    while bit <= mask:
        if mask & bit:
            value = value + bit * (1 - 2 * lax.rem(lax.div(value, bit), 2))
        bit *= 2
    return value


def masks_above(bit, planes):
    return [m for m in range(planes) if m % (2 * bit) == 0]


def window_kernel(
    planes, across, shards, aligned,
    ids, coefs, x_ref, g_ref, up_ref, down_ref, came_up, came_down,
    relay0, relay1, relay2, relay3, stage, weights, back, norm1, norm2, cot, backmid, hid1, hid2, backpre,
    slope1, slope2, part, outgoing, incoming, own_x, middle,
    z_send, z_recv, p_send, p_recv, g_send, g_recv, m_send, m_recv,
    a_send, a_recv, r_send, r_recv, t_send, t_recv, local_z, local_m,
):
    relay = (relay0, relay1, relay2, relay3)
    path = lax.axis_index("path")
    shard = lax.axis_index("fsdp")
    plane = lax.div(path, across)
    column = lax.rem(path, across)
    slots = across * shards
    slot = column * shards + shard
    rows, depth = x_ref.shape
    half, piece, narrow = relay0.shape[1:]
    width = narrow * shards * planes
    in_scale = 1.0 / math.sqrt(depth)
    hid_scale = 1.0 / math.sqrt(width)
    bf16, f32 = jnp.bfloat16, jnp.float32
    bits = [1 << b for b in range(planes.bit_length() - 1)]

    def block(at):
        return pl.ds(pl.multiple_of(at * rows, rows), rows)

    def in_plane(to):
        return (plane * across + lax.div(to, shards), lax.rem(to, shards))

    def along(to):
        return (to * across + column, shard)

    def quarter(ref, level, at):
        if aligned:
            return ref.at[
                pl.ds(level * half, half), :, pl.ds(pl.multiple_of(at * narrow, narrow), narrow)
            ]
        return ref.at[at, pl.ds(level * half, half)]

    def remote(src, dst, send, recv, to):
        return pltpu.make_async_remote_copy(
            src_ref=src, dst_ref=dst, send_sem=send, recv_sem=recv,
            device_id=to, device_id_type=MESH,
        )

    def z_copy(k, j, to):
        source = (up_ref, down_ref)[k % 2]
        return remote(quarter(source, k // 2, to), relay[k].at[plane],
                      z_send.at[k, j], z_recv.at[k, j], along(to))

    def z_own(k):
        source = (up_ref, down_ref)[k % 2]
        return pltpu.make_async_copy(
            quarter(source, k // 2, plane), relay[k].at[plane], local_z.at[k])

    def z_start(k):
        loop(1, planes, lambda j: z_copy(k, j, lax.rem(plane + j, planes)).start())

    def z_wait(k):
        def act(j):
            origin = lax.rem(plane + planes - j, planes)
            remote(relay[k].at[origin], relay[k].at[origin],
                   z_send.at[k, j], z_recv.at[k, j], along(origin)).wait_recv()

        loop(1, planes, act)
        z_own(k).wait()

    def p_copy(k, j, to):
        return remote(stage.at[k, to], weights.at[k, shard, :, column],
                      p_send.at[k, j], p_recv.at[k, j], in_plane(to))

    def p_start(k):
        def act(j):
            to = lax.rem(slot + j, slots)
            stage[k, to] = relay[k][:, ids[(k // 2) * slots + to]]
            p_copy(k, j, to).start()

        loop(1, slots, act)
        weights[k, shard, :, column] = relay[k][:, ids[(k // 2) * slots + slot]]

    def p_wait(k):
        def act(j):
            origin = lax.rem(slot + slots - j, slots)
            land = weights.at[k, lax.rem(origin, shards), :, lax.div(origin, shards)]
            remote(land, land, p_send.at[k, j], p_recv.at[k, j], in_plane(origin)).wait_recv()

        loop(1, slots, act)

    def p_sent(k):
        loop(1, slots, lambda j: p_copy(k, j, lax.rem(slot + j, slots)).wait_send())

    def weight(k, at):
        return weights[k, at].reshape(depth, narrow)

    def g_copy(k, j, to):
        return remote(stage.at[k, to], back.at[k, slot],
                      g_send.at[k, j], g_recv.at[k, j], in_plane(to))

    def g_start(k, left, right, factor):
        p_sent(k)

        def act(at):
            value = inner_rate * (dot(left[...], right[at], ((0,), (0,))) * factor)
            value = value.astype(bf16).reshape(planes, across, piece, narrow)
            for c in range(across):
                stage[k, c * shards + at] = value[:, c]

        loop(0, shards, act)
        loop(1, slots, lambda j: g_copy(k, j, lax.rem(slot + j, slots)).start())
        back[k, slot] = stage[k, slot]

    def g_wait(k):
        def act(j):
            origin = lax.rem(slot + slots - j, slots)
            remote(back.at[k, origin], back.at[k, origin],
                   g_send.at[k, j], g_recv.at[k, j], in_plane(origin)).wait_recv()

        loop(1, slots, act)

    def m_copy(k, j, to):
        target = (came_up, came_down)[k % 2]
        return remote(relay[k].at[to], quarter(target, k // 2, plane),
                      m_send.at[k, j], m_recv.at[k, j], along(to))

    def m_own(k):
        target = (came_up, came_down)[k % 2]
        return pltpu.make_async_copy(
            relay[k].at[plane], quarter(target, k // 2, plane), local_m.at[k])

    def m_start(k):
        g_wait(k)
        strip = 32
        strips = piece // strip
        batch = min(4, half)

        def act(at):
            to = lax.div(at, strips)
            lines = pl.ds(pl.multiple_of(lax.rem(at, strips) * strip, strip), strip)
            for first in range(0, half, batch):
                totals = [jnp.zeros((strip, narrow), f32)] * batch
                for t in range(slots):
                    value = back[k, t, to, lines, :].astype(f32)
                    totals = [
                        total + coefs[((k // 2) * half + first + m) * slots + t] * value
                        for m, total in enumerate(totals)
                    ]
                for m, total in enumerate(totals):
                    relay[k][to, first + m, lines, :] = total.astype(bf16)

        loop(0, planes * strips, act)
        loop(1, planes, lambda j: m_copy(k, j, lax.rem(plane + j, planes)).start())
        m_own(k).start()

    def m_wait(k):
        target = (came_up, came_down)[k % 2]

        def act(j):
            origin = lax.rem(plane + planes - j, planes)
            land = quarter(target, k // 2, origin)
            remote(land, land, m_send.at[k, j], m_recv.at[k, j], along(origin)).wait_recv()

        loop(1, planes, act)
        m_own(k).wait()

    gather_plan = []
    for bit in reversed(bits):
        for mask in masks_above(bit, planes):
            gather_plan.append((bit, mask))

    def a_copy(i, buf, c):
        bit, mask = gather_plan[c]
        at = block(flipped(plane, mask))
        return remote(buf.at[at], buf.at[at], a_send.at[i, c], a_recv.at[i, c],
                      along(flipped(plane, bit)))

    def a_start(i, buf, bit):
        for c, step in enumerate(gather_plan):
            if step[0] == bit:
                a_copy(i, buf, c).start()

    def a_wait(i, buf, bit):
        for c, step in enumerate(gather_plan):
            if step[0] == bit:
                at = block(flipped(flipped(plane, bit), step[1]))
                remote(buf.at[at], buf.at[at], a_send.at[i, c], a_recv.at[i, c],
                       along(flipped(plane, bit))).wait_recv()

    def a_through(i, buf):
        for bit in reversed(bits[1:]):
            a_start(i, buf, bit)
            a_wait(i, buf, bit)
        a_start(i, buf, 1)

    sum_plan = []
    for bit in bits:
        for mask in masks_above(bit, planes):
            sum_plan.append((bit, mask))

    def r_copy(i, c):
        return remote(outgoing.at[c], incoming.at[i % incoming.shape[0], c], r_send.at[i, c], r_recv.at[i, c],
                      along(flipped(plane, sum_plan[c][0])))

    def products(left, k, factor):
        def act(at):
            total = dot(left[0, block(at), :], weight(k, 0), ((1,), (1,)))
            for c in range(1, shards):
                total = total + dot(left[c, block(at), :], weight(k, c), ((1,), (1,)))
            part[at] = total * factor

        loop(0, planes, act)

    def r_start(i, bit):
        for c, (of, mask) in enumerate(sum_plan):
            if of == bit:
                outgoing[c] = part[flipped(flipped(plane, bit), mask)].astype(bf16)
                r_copy(i, c).start()

    def r_wait(i, bit):
        for c, (of, mask) in enumerate(sum_plan):
            if of == bit:
                r_copy(i, c).wait_recv()
                at = flipped(plane, mask)
                part[at] = part[at] + incoming[i % incoming.shape[0], c].astype(f32)

    def r_through(i):
        for bit in bits[1:]:
            r_start(i, bit)
            r_wait(i, bit)
        return part[plane]

    token_to = (shard * across + lax.div(path, shards), lax.rem(path, shards))
    token_from = (slot, plane)
    away = jnp.logical_or(token_to[0] != path, token_to[1] != shard)

    def t_copy(i, to, at):
        land = (own_x, cot.at[block(at)])[i]
        return remote((x_ref, g_ref)[i], land, t_send.at[i], t_recv.at[i], to)

    def greet(to):
        pl.semaphore_signal(barrier, inc=1, device_id=to, device_id_type=MESH)

    barrier = pltpu.get_barrier_semaphore()
    loop(1, planes, lambda j: greet(along(lax.rem(plane + j, planes))))
    loop(1, slots, lambda j: greet(in_plane(lax.rem(slot + j, slots))))

    @pl.when(away)
    def _():
        greet(token_to)
        greet(token_from)
        pl.semaphore_wait(barrier, planes + slots)
        t_copy(0, token_to, shard).start()

    @pl.when(jnp.logical_not(away))
    def _():
        pl.semaphore_wait(barrier, planes + slots - 2)

    z_start(0)

    @pl.when(away)
    def _():
        t_copy(1, token_to, shard).start()

    for k in range(4):
        z_own(k).start()

    @pl.when(away)
    def _():
        t_copy(0, token_from, plane).wait_recv()

    @pl.when(jnp.logical_not(away))
    def _():
        own_x[...] = x_ref[...]
        cot[block(plane), :] = g_ref[...]

    tokens = own_x[...].astype(f32)
    norm1[block(plane), :] = (tokens * row_scale(tokens)).astype(bf16)
    a_start(0, norm1, bits[-1])
    z_start(1)
    a_wait(0, norm1, bits[-1])
    for bit in reversed(bits[:-1]):
        a_start(0, norm1, bit)
        if bit > 1:
            a_wait(0, norm1, bit)

    @pl.when(away)
    def _():
        t_copy(1, token_from, plane).wait_recv()

    z_wait(0)
    z_start(2)
    p_start(0)
    a_start(1, cot, bits[-1])
    z_wait(1)
    z_start(3)
    p_start(1)
    a_wait(1, cot, bits[-1])
    for bit in reversed(bits[:-1]):
        a_start(1, cot, bit)
        if bit > 1:
            a_wait(1, cot, bit)
    a_wait(0, norm1, 1)
    p_wait(0)

    def forward_first(at):
        value, slope = gelu_both(dot(norm1[...], weight(0, at)) * in_scale)
        hid1[at] = value.astype(bf16)
        slope1[at] = slope

    loop(0, shards, forward_first)
    z_wait(2)
    p_start(2)
    p_wait(1)
    products(hid1, 1, hid_scale)
    r_start(0, 1)
    r_wait(0, 1)
    mid = own_x[...].astype(f32) + r_through(0)
    middle[...] = mid
    norm2[block(plane), :] = (mid * row_scale(mid)).astype(bf16)
    a_through(2, norm2)
    z_wait(3)
    p_start(3)
    a_wait(2, norm2, 1)
    p_wait(2)

    def forward_second(at):
        value, slope = gelu_both(dot(norm2[...], weight(2, at)) * in_scale)
        hid2[at] = value.astype(bf16)
        slope2[at] = slope

    loop(0, shards, forward_second)
    a_wait(1, cot, 1)
    p_wait(3)

    def back_second(at):
        value = dot(cot[...], weight(3, at)) * hid_scale
        backpre[at] = (value * slope2[at]).astype(bf16)

    loop(0, shards, back_second)
    products(backpre, 2, in_scale)
    for c in range(planes - 1):
        r_copy(0, c).wait_send()
    r_start(1, 1)
    g_start(3, cot, hid2, hid_scale)
    r_wait(1, 1)
    if len(bits) > 1:
        r_start(1, bits[1])
    g_start(2, norm2, backpre, in_scale)
    for bit in bits[1:]:
        r_wait(1, bit)
        if bit != bits[-1]:
            r_start(1, 2 * bit)
    back_normed = part[plane]
    mid = middle[...]
    scale = row_scale(mid)
    unit = mid * scale
    centred = back_normed - unit * jnp.mean(back_normed * unit, axis=-1, keepdims=True)
    backmid[block(plane), :] = (cot[block(plane), :].astype(f32) + scale * centred).astype(bf16)
    a_through(3, backmid)
    a_wait(3, backmid, 1)
    g_start(1, backmid, hid1, hid_scale)

    def back_first(at):
        value = dot(backmid[...], weight(1, at)) * hid_scale
        backpre[at] = (value * slope1[at]).astype(bf16)

    loop(0, shards, back_first)
    g_start(0, norm1, backpre, in_scale)
    for k in (3, 2, 1, 0):
        if k > 1:
            loop(1, planes, lambda j: z_copy(k, j, lax.rem(plane + j, planes)).wait_send())
        m_start(k)
    for k in (3, 2, 1, 0):
        m_wait(k)

    for k in range(4):
        if k < 2:
            loop(1, planes, lambda j: z_copy(k, j, lax.rem(plane + j, planes)).wait_send())
        loop(1, planes, lambda j: m_copy(k, j, lax.rem(plane + j, planes)).wait_send())
        loop(1, slots, lambda j: g_copy(k, j, lax.rem(slot + j, slots)).wait_send())
    for i, buf in enumerate((norm1, cot, norm2, backmid)):
        for c in range(planes - 1):
            a_copy(i, buf, c).wait_send()
    for c in range(planes - 1):
        r_copy(1, c).wait_send()

    @pl.when(away)
    def _():
        t_copy(0, token_to, shard).wait_send()
        t_copy(1, token_to, shard).wait_send()


def window(planes, across, shards, aligned, ids, coefs, tokens, cotangent, up, down):
    half = coefs.shape[0] // (2 * across * shards)
    slots = across * shards
    piece = up.shape[-2]
    narrow = up.shape[-1] // planes if aligned else up.shape[-1]
    rows, depth = tokens.shape
    total = rows * shards
    bf16, f32 = jnp.bfloat16, jnp.float32
    vmem = pl.BlockSpec(memory_space=pltpu.VMEM)
    smem = pl.BlockSpec(memory_space=pltpu.SMEM)
    anywhere = pl.BlockSpec(memory_space=pl.ANY)
    dma = pltpu.SemaphoreType.DMA
    out = jax.ShapeDtypeStruct(up.shape, bf16)
    return pl.pallas_call(
        functools.partial(window_kernel, planes, across, shards, aligned),
        out_shape=(out, out),
        in_specs=[smem, smem, vmem, vmem, anywhere, anywhere],
        out_specs=(anywhere, anywhere),
        scratch_shapes=[
            *[pltpu.VMEM((planes, half, piece, narrow), bf16)] * 4,
            pltpu.VMEM((4, slots, planes, piece, narrow), bf16),
            pltpu.VMEM((4, shards, planes, across, piece, narrow), bf16),
            pltpu.VMEM((4, slots, planes, piece, narrow), bf16),
            pltpu.VMEM((total, depth), bf16),
            pltpu.VMEM((total, depth), bf16),
            pltpu.VMEM((total, depth), bf16),
            pltpu.VMEM((total, depth), bf16),
            pltpu.VMEM((shards, total, narrow), bf16),
            pltpu.VMEM((shards, total, narrow), bf16),
            pltpu.VMEM((shards, total, narrow), bf16),
            pltpu.VMEM((shards, total, narrow), f32),
            pltpu.VMEM((shards, total, narrow), f32),
            pltpu.VMEM((planes, rows, depth), f32),
            pltpu.VMEM((planes - 1, rows, depth), bf16),
            pltpu.VMEM((1 + aligned, planes - 1, rows, depth), bf16),
            pltpu.VMEM((rows, depth), bf16),
            pltpu.VMEM((rows, depth), f32),
            dma((4, planes)), dma((4, planes)),
            dma((4, slots)), dma((4, slots)),
            dma((4, slots)), dma((4, slots)),
            dma((4, planes)), dma((4, planes)),
            dma((4, planes)), dma((4, planes)),
            dma((2, planes)), dma((2, planes)),
            dma((2,)), dma((2,)),
            dma((4,)), dma((4,)),
        ],
        compiler_params=pltpu.CompilerParams(
            collective_id=0, has_side_effects=True, vmem_limit_bytes=61 * 1024 * 1024
        ),
        cost_estimate=pl.CostEstimate(
            flops=20 * total * depth * narrow * shards,
            bytes_accessed=16 * depth * narrow * shards,
            transcendentals=2 * total * narrow * shards,
        ),
        name="window",
    )(ids, coefs, tokens, cotangent, up, down)


def outer_step(weight, moment, mean):
    mean = mean.astype(jnp.float32)
    fresh = keep_rate * moment.astype(jnp.float32) + mean
    step = weight.astype(jnp.float32) - outer_rate * (mean + keep_rate * fresh)
    return step.astype(jnp.bfloat16), fresh.astype(jnp.bfloat16)


def body(paths, shards, hidden_in, cotangent, up_weight, down_weight, up_moment, down_moment, sharing):
    modules, piece, cols = up_weight.shape
    planes = shards
    across = paths // planes
    narrow = cols // planes
    aligned = narrow % 128 == 0
    half = modules // 2
    owners = jnp.transpose(sharing)
    ids = (owners - jnp.array([[0], [half]], jnp.int32)).reshape(-1)
    level = jnp.repeat(owners, half, axis=0)
    member = (level == jnp.arange(modules, dtype=jnp.int32)[:, None]).astype(jnp.float32)
    coefs = (member / jnp.sum(member, axis=1, keepdims=True)).reshape(-1)
    up, down = up_weight, down_weight
    if not aligned:
        up, down = (
            jnp.transpose(v.reshape(modules, piece, planes, narrow), (2, 0, 1, 3))
            for v in (up, down)
        )
    mean_up, mean_down = window(
        planes, across, shards, aligned, ids, coefs, hidden_in[0], cotangent[0], up, down
    )
    if not aligned:
        mean_up, mean_down = (
            jnp.transpose(v, (1, 2, 0, 3)).reshape(modules, piece, cols)
            for v in (mean_up, mean_down)
        )
    new_up, new_up_moment = outer_step(up_weight, up_moment, mean_up)
    new_down, new_down_moment = outer_step(down_weight, down_moment, mean_down)
    return (new_up, new_down, new_up_moment, new_down_moment)


def solution(mesh):
    weights = P(None, "path", "fsdp")
    tokens = P("path", "fsdp", None)
    return jax.shard_map(
        functools.partial(body, mesh.shape["path"], mesh.shape["fsdp"]),
        mesh=mesh,
        in_specs=(tokens, tokens, weights, weights, weights, weights, P()),
        out_specs=(weights,) * 4,
        check_vma=False,
    )
```

```python
import functools
import math

import jax
import jax.numpy as jnp
from jax import lax
from jax.experimental import pallas as pl
from jax.experimental.pallas import tpu as pltpu
from jax.sharding import PartitionSpec as P

inner_rate = 2.0
outer_rate = 0.7
keep_rate = 0.9
norm_eps = 1e-06
tanh_coeff = 0.7978845608028654
cube_coeff = 0.044715
MESH = pl.DeviceIdType.MESH


def gelu_both(values):
    inside = tanh_coeff * (values + cube_coeff * values * values * values)
    tangent = jnp.tanh(inside)
    value = 0.5 * values * (1.0 + tangent)
    slope = 0.5 * (1.0 + tangent) + 0.5 * values * (1.0 - tangent * tangent) * tanh_coeff * (
        1.0 + 3.0 * cube_coeff * values * values
    )
    return value, slope


def row_scale(values):
    return lax.rsqrt(jnp.mean(values * values, axis=-1, keepdims=True) + norm_eps)


def dot(left, right, dims=((1,), (0,))):
    return lax.dot_general(left, right, (dims, ((), ())), preferred_element_type=jnp.float32)


def loop(first, count, act):
    def step(j, carry):
        act(j)
        return carry

    lax.fori_loop(first, count, step, 0)


def flipped(value, mask):
    bit = 1
    while bit <= mask:
        if mask & bit:
            value = value + bit * (1 - 2 * lax.rem(lax.div(value, bit), 2))
        bit *= 2
    return value


def masks_above(bit, planes):
    return [m for m in range(planes) if m % (2 * bit) == 0]


def window_kernel(
    planes, across, shards, aligned,
    ids, coefs, x_ref, g_ref, up_ref, down_ref, came_up, came_down,
    relay0, relay1, relay2, relay3, stage, weights, back, norm1, norm2, cot, backmid, hid1, hid2, backpre,
    slope1, slope2, part, outgoing, incoming, own_x, middle,
    z_send, z_recv, p_send, p_recv, g_send, g_recv, m_send, m_recv,
    a_send, a_recv, r_send, r_recv, t_send, t_recv, local_z, local_m,
):
    relay = (relay0, relay1, relay2, relay3)
    path = lax.axis_index("path")
    shard = lax.axis_index("fsdp")
    plane = lax.div(path, across)
    column = lax.rem(path, across)
    slots = across * shards
    slot = column * shards + shard
    rows, depth = x_ref.shape
    half, piece, narrow = relay0.shape[1:]
    width = narrow * shards * planes
    in_scale = 1.0 / math.sqrt(depth)
    hid_scale = 1.0 / math.sqrt(width)
    bf16, f32 = jnp.bfloat16, jnp.float32
    bits = [1 << b for b in range(planes.bit_length() - 1)]

    def block(at):
        return pl.ds(pl.multiple_of(at * rows, rows), rows)

    def in_plane(to):
        return (plane * across + lax.div(to, shards), lax.rem(to, shards))

    def along(to):
        return (to * across + column, shard)

    def quarter(ref, level, at):
        if aligned:
            return ref.at[
                pl.ds(level * half, half), :, pl.ds(pl.multiple_of(at * narrow, narrow), narrow)
            ]
        return ref.at[at, pl.ds(level * half, half)]

    def remote(src, dst, send, recv, to):
        return pltpu.make_async_remote_copy(
            src_ref=src, dst_ref=dst, send_sem=send, recv_sem=recv,
            device_id=to, device_id_type=MESH,
        )

    def z_copy(k, j, to):
        source = (up_ref, down_ref)[k % 2]
        return remote(quarter(source, k // 2, to), relay[k].at[plane],
                      z_send.at[k, j], z_recv.at[k, j], along(to))

    def z_own(k):
        source = (up_ref, down_ref)[k % 2]
        return pltpu.make_async_copy(
            quarter(source, k // 2, plane), relay[k].at[plane], local_z.at[k])

    def z_start(k):
        loop(1, planes, lambda j: z_copy(k, j, lax.rem(plane + j, planes)).start())

    def z_wait(k):
        def act(j):
            origin = lax.rem(plane + planes - j, planes)
            remote(relay[k].at[origin], relay[k].at[origin],
                   z_send.at[k, j], z_recv.at[k, j], along(origin)).wait_recv()

        loop(1, planes, act)
        z_own(k).wait()

    def p_copy(k, j, to):
        return remote(stage.at[k, to], weights.at[k, shard, :, column],
                      p_send.at[k, j], p_recv.at[k, j], in_plane(to))

    def p_start(k):
        def act(j):
            to = lax.rem(slot + j, slots)
            stage[k, to] = relay[k][:, ids[(k // 2) * slots + to]]
            p_copy(k, j, to).start()

        loop(1, slots, act)
        weights[k, shard, :, column] = relay[k][:, ids[(k // 2) * slots + slot]]

    def p_wait(k):
        def act(j):
            origin = lax.rem(slot + slots - j, slots)
            land = weights.at[k, lax.rem(origin, shards), :, lax.div(origin, shards)]
            remote(land, land, p_send.at[k, j], p_recv.at[k, j], in_plane(origin)).wait_recv()

        loop(1, slots, act)

    def p_sent(k):
        loop(1, slots, lambda j: p_copy(k, j, lax.rem(slot + j, slots)).wait_send())

    def weight(k, at):
        return weights[k, at].reshape(depth, narrow)

    def g_copy(k, j, to):
        return remote(stage.at[k, to], back.at[k, slot],
                      g_send.at[k, j], g_recv.at[k, j], in_plane(to))

    def g_start(k, left, right, factor):
        p_sent(k)

        def act(at):
            value = inner_rate * (dot(left[...], right[at], ((0,), (0,))) * factor)
            value = value.astype(bf16).reshape(planes, across, piece, narrow)
            for c in range(across):
                stage[k, c * shards + at] = value[:, c]

        loop(0, shards, act)
        loop(1, slots, lambda j: g_copy(k, j, lax.rem(slot + j, slots)).start())
        back[k, slot] = stage[k, slot]

    def g_wait(k):
        def act(j):
            origin = lax.rem(slot + slots - j, slots)
            remote(back.at[k, origin], back.at[k, origin],
                   g_send.at[k, j], g_recv.at[k, j], in_plane(origin)).wait_recv()

        loop(1, slots, act)

    def m_copy(k, j, to):
        target = (came_up, came_down)[k % 2]
        return remote(relay[k].at[to], quarter(target, k // 2, plane),
                      m_send.at[k, j], m_recv.at[k, j], along(to))

    def m_own(k):
        target = (came_up, came_down)[k % 2]
        return pltpu.make_async_copy(
            relay[k].at[plane], quarter(target, k // 2, plane), local_m.at[k])

    def m_start(k):
        g_wait(k)
        strip = 32
        strips = piece // strip
        batch = min(4, half)

        def act(at):
            to = lax.div(at, strips)
            lines = pl.ds(pl.multiple_of(lax.rem(at, strips) * strip, strip), strip)
            for first in range(0, half, batch):
                totals = [jnp.zeros((strip, narrow), f32)] * batch
                for t in range(slots):
                    value = back[k, t, to, lines, :].astype(f32)
                    totals = [
                        total + coefs[((k // 2) * half + first + m) * slots + t] * value
                        for m, total in enumerate(totals)
                    ]
                for m, total in enumerate(totals):
                    relay[k][to, first + m, lines, :] = total.astype(bf16)

        loop(0, planes * strips, act)
        loop(1, planes, lambda j: m_copy(k, j, lax.rem(plane + j, planes)).start())
        m_own(k).start()

    def m_wait(k):
        target = (came_up, came_down)[k % 2]

        def act(j):
            origin = lax.rem(plane + planes - j, planes)
            land = quarter(target, k // 2, origin)
            remote(land, land, m_send.at[k, j], m_recv.at[k, j], along(origin)).wait_recv()

        loop(1, planes, act)
        m_own(k).wait()

    gather_plan = []
    for bit in reversed(bits):
        for mask in masks_above(bit, planes):
            gather_plan.append((bit, mask))

    def a_copy(i, buf, c):
        bit, mask = gather_plan[c]
        at = block(flipped(plane, mask))
        return remote(buf.at[at], buf.at[at], a_send.at[i, c], a_recv.at[i, c],
                      along(flipped(plane, bit)))

    def a_start(i, buf, bit):
        for c, step in enumerate(gather_plan):
            if step[0] == bit:
                a_copy(i, buf, c).start()

    def a_wait(i, buf, bit):
        for c, step in enumerate(gather_plan):
            if step[0] == bit:
                at = block(flipped(flipped(plane, bit), step[1]))
                remote(buf.at[at], buf.at[at], a_send.at[i, c], a_recv.at[i, c],
                       along(flipped(plane, bit))).wait_recv()

    def a_through(i, buf):
        for bit in reversed(bits[1:]):
            a_start(i, buf, bit)
            a_wait(i, buf, bit)
        a_start(i, buf, 1)

    sum_plan = []
    for bit in bits:
        for mask in masks_above(bit, planes):
            sum_plan.append((bit, mask))

    def r_copy(i, c):
        return remote(outgoing.at[c], incoming.at[i % incoming.shape[0], c], r_send.at[i, c], r_recv.at[i, c],
                      along(flipped(plane, sum_plan[c][0])))

    def products(left, k, factor):
        def act(at):
            total = dot(left[0, block(at), :], weight(k, 0), ((1,), (1,)))
            for c in range(1, shards):
                total = total + dot(left[c, block(at), :], weight(k, c), ((1,), (1,)))
            part[at] = total * factor

        loop(0, planes, act)

    def r_start(i, bit):
        for c, (of, mask) in enumerate(sum_plan):
            if of == bit:
                outgoing[c] = part[flipped(flipped(plane, bit), mask)].astype(bf16)
                r_copy(i, c).start()

    def r_wait(i, bit):
        for c, (of, mask) in enumerate(sum_plan):
            if of == bit:
                r_copy(i, c).wait_recv()
                at = flipped(plane, mask)
                part[at] = part[at] + incoming[i % incoming.shape[0], c].astype(f32)

    def r_through(i):
        for bit in bits[1:]:
            r_start(i, bit)
            r_wait(i, bit)
        return part[plane]

    token_to = (shard * across + lax.div(path, shards), lax.rem(path, shards))
    token_from = (slot, plane)
    away = jnp.logical_or(token_to[0] != path, token_to[1] != shard)

    def t_copy(i, to, at):
        land = (own_x, cot.at[block(at)])[i]
        return remote((x_ref, g_ref)[i], land, t_send.at[i], t_recv.at[i], to)

    def greet(to):
        pl.semaphore_signal(barrier, inc=1, device_id=to, device_id_type=MESH)

    barrier = pltpu.get_barrier_semaphore()
    loop(1, planes, lambda j: greet(along(lax.rem(plane + j, planes))))
    loop(1, slots, lambda j: greet(in_plane(lax.rem(slot + j, slots))))

    @pl.when(away)
    def _():
        greet(token_to)
        greet(token_from)
        pl.semaphore_wait(barrier, planes + slots)
        t_copy(0, token_to, shard).start()

    @pl.when(jnp.logical_not(away))
    def _():
        pl.semaphore_wait(barrier, planes + slots - 2)

    z_start(0)

    @pl.when(away)
    def _():
        t_copy(1, token_to, shard).start()

    for k in range(4):
        z_own(k).start()

    @pl.when(away)
    def _():
        t_copy(0, token_from, plane).wait_recv()

    @pl.when(jnp.logical_not(away))
    def _():
        own_x[...] = x_ref[...]
        cot[block(plane), :] = g_ref[...]

    tokens = own_x[...].astype(f32)
    norm1[block(plane), :] = (tokens * row_scale(tokens)).astype(bf16)
    a_start(0, norm1, bits[-1])
    a_wait(0, norm1, bits[-1])
    for bit in reversed(bits[:-1]):
        a_start(0, norm1, bit)
        if bit > 1:
            a_wait(0, norm1, bit)

    @pl.when(away)
    def _():
        t_copy(1, token_from, plane).wait_recv()

    z_wait(0)
    z_start(1)
    p_start(0)
    a_start(1, cot, bits[-1])
    z_wait(1)
    z_start(2)
    p_start(1)
    a_wait(1, cot, bits[-1])
    for bit in reversed(bits[:-1]):
        a_start(1, cot, bit)
        if bit > 1:
            a_wait(1, cot, bit)
    a_wait(0, norm1, 1)
    p_wait(0)

    def forward_first(at):
        value, slope = gelu_both(dot(norm1[...], weight(0, at)) * in_scale)
        hid1[at] = value.astype(bf16)
        slope1[at] = slope

    loop(0, shards, forward_first)
    p_wait(1)
    products(hid1, 1, hid_scale)
    r_start(0, 1)
    z_wait(2)
    z_start(3)
    p_start(2)
    r_wait(0, 1)
    mid = own_x[...].astype(f32) + r_through(0)
    middle[...] = mid
    norm2[block(plane), :] = (mid * row_scale(mid)).astype(bf16)
    a_through(2, norm2)
    z_wait(3)
    p_start(3)
    a_wait(2, norm2, 1)
    p_wait(2)

    def forward_second(at):
        value, slope = gelu_both(dot(norm2[...], weight(2, at)) * in_scale)
        hid2[at] = value.astype(bf16)
        slope2[at] = slope

    loop(0, shards, forward_second)
    a_wait(1, cot, 1)
    p_wait(3)

    def back_second(at):
        value = dot(cot[...], weight(3, at)) * hid_scale
        backpre[at] = (value * slope2[at]).astype(bf16)

    loop(0, shards, back_second)
    products(backpre, 2, in_scale)
    for c in range(planes - 1):
        r_copy(0, c).wait_send()
    r_start(1, 1)
    g_start(3, cot, hid2, hid_scale)
    r_wait(1, 1)
    if len(bits) > 1:
        r_start(1, bits[1])
    g_start(2, norm2, backpre, in_scale)
    for bit in bits[1:]:
        r_wait(1, bit)
        if bit != bits[-1]:
            r_start(1, 2 * bit)
    back_normed = part[plane]
    mid = middle[...]
    scale = row_scale(mid)
    unit = mid * scale
    centred = back_normed - unit * jnp.mean(back_normed * unit, axis=-1, keepdims=True)
    backmid[block(plane), :] = (cot[block(plane), :].astype(f32) + scale * centred).astype(bf16)
    a_through(3, backmid)
    loop(1, planes, lambda j: z_copy(3, j, lax.rem(plane + j, planes)).wait_send())
    m_start(3)
    a_wait(3, backmid, 1)
    g_start(1, backmid, hid1, hid_scale)

    def back_first(at):
        value = dot(backmid[...], weight(1, at)) * hid_scale
        backpre[at] = (value * slope1[at]).astype(bf16)

    loop(0, shards, back_first)
    g_start(0, norm1, backpre, in_scale)
    for k in (2, 1, 0):
        m_start(k)
    for k in (3, 2, 1, 0):
        m_wait(k)

    for k in range(4):
        if k < 3:
            loop(1, planes, lambda j: z_copy(k, j, lax.rem(plane + j, planes)).wait_send())
        loop(1, planes, lambda j: m_copy(k, j, lax.rem(plane + j, planes)).wait_send())
        loop(1, slots, lambda j: g_copy(k, j, lax.rem(slot + j, slots)).wait_send())
    for i, buf in enumerate((norm1, cot, norm2, backmid)):
        for c in range(planes - 1):
            a_copy(i, buf, c).wait_send()
    for c in range(planes - 1):
        r_copy(1, c).wait_send()

    @pl.when(away)
    def _():
        t_copy(0, token_to, shard).wait_send()
        t_copy(1, token_to, shard).wait_send()


def window(planes, across, shards, aligned, ids, coefs, tokens, cotangent, up, down):
    half = coefs.shape[0] // (2 * across * shards)
    slots = across * shards
    piece = up.shape[-2]
    narrow = up.shape[-1] // planes if aligned else up.shape[-1]
    rows, depth = tokens.shape
    total = rows * shards
    bf16, f32 = jnp.bfloat16, jnp.float32
    vmem = pl.BlockSpec(memory_space=pltpu.VMEM)
    smem = pl.BlockSpec(memory_space=pltpu.SMEM)
    anywhere = pl.BlockSpec(memory_space=pl.ANY)
    dma = pltpu.SemaphoreType.DMA
    out = jax.ShapeDtypeStruct(up.shape, bf16)
    return pl.pallas_call(
        functools.partial(window_kernel, planes, across, shards, aligned),
        out_shape=(out, out),
        in_specs=[smem, smem, vmem, vmem, anywhere, anywhere],
        out_specs=(anywhere, anywhere),
        scratch_shapes=[
            *[pltpu.VMEM((planes, half, piece, narrow), bf16)] * 4,
            pltpu.VMEM((4, slots, planes, piece, narrow), bf16),
            pltpu.VMEM((4, shards, planes, across, piece, narrow), bf16),
            pltpu.VMEM((4, slots, planes, piece, narrow), bf16),
            pltpu.VMEM((total, depth), bf16),
            pltpu.VMEM((total, depth), bf16),
            pltpu.VMEM((total, depth), bf16),
            pltpu.VMEM((total, depth), bf16),
            pltpu.VMEM((shards, total, narrow), bf16),
            pltpu.VMEM((shards, total, narrow), bf16),
            pltpu.VMEM((shards, total, narrow), bf16),
            pltpu.VMEM((shards, total, narrow), f32),
            pltpu.VMEM((shards, total, narrow), f32),
            pltpu.VMEM((planes, rows, depth), f32),
            pltpu.VMEM((planes - 1, rows, depth), bf16),
            pltpu.VMEM((1 + aligned, planes - 1, rows, depth), bf16),
            pltpu.VMEM((rows, depth), bf16),
            pltpu.VMEM((rows, depth), f32),
            dma((4, planes)), dma((4, planes)),
            dma((4, slots)), dma((4, slots)),
            dma((4, slots)), dma((4, slots)),
            dma((4, planes)), dma((4, planes)),
            dma((4, planes)), dma((4, planes)),
            dma((2, planes)), dma((2, planes)),
            dma((2,)), dma((2,)),
            dma((4,)), dma((4,)),
        ],
        compiler_params=pltpu.CompilerParams(
            collective_id=0, has_side_effects=True, vmem_limit_bytes=61 * 1024 * 1024
        ),
        cost_estimate=pl.CostEstimate(
            flops=20 * total * depth * narrow * shards,
            bytes_accessed=16 * depth * narrow * shards,
            transcendentals=2 * total * narrow * shards,
        ),
        name="window",
    )(ids, coefs, tokens, cotangent, up, down)


def outer_step(weight, moment, mean):
    mean = mean.astype(jnp.float32)
    fresh = keep_rate * moment.astype(jnp.float32) + mean
    step = weight.astype(jnp.float32) - outer_rate * (mean + keep_rate * fresh)
    return step.astype(jnp.bfloat16), fresh.astype(jnp.bfloat16)


def body(paths, shards, hidden_in, cotangent, up_weight, down_weight, up_moment, down_moment, sharing):
    modules, piece, cols = up_weight.shape
    planes = shards
    across = paths // planes
    narrow = cols // planes
    aligned = narrow % 128 == 0
    half = modules // 2
    owners = jnp.transpose(sharing)
    ids = (owners - jnp.array([[0], [half]], jnp.int32)).reshape(-1)
    level = jnp.repeat(owners, half, axis=0)
    member = (level == jnp.arange(modules, dtype=jnp.int32)[:, None]).astype(jnp.float32)
    coefs = (member / jnp.sum(member, axis=1, keepdims=True)).reshape(-1)
    up, down = up_weight, down_weight
    if not aligned:
        up, down = (
            jnp.transpose(v.reshape(modules, piece, planes, narrow), (2, 0, 1, 3))
            for v in (up, down)
        )
    mean_up, mean_down = window(
        planes, across, shards, aligned, ids, coefs, hidden_in[0], cotangent[0], up, down
    )
    if not aligned:
        mean_up, mean_down = (
            jnp.transpose(v, (1, 2, 0, 3)).reshape(modules, piece, cols)
            for v in (mean_up, mean_down)
        )
    new_up, new_up_moment = outer_step(up_weight, up_moment, mean_up)
    new_down, new_down_moment = outer_step(down_weight, down_moment, mean_down)
    return (new_up, new_down, new_up_moment, new_down_moment)


def solution(mesh):
    weights = P(None, "path", "fsdp")
    tokens = P("path", "fsdp", None)
    return jax.shard_map(
        functools.partial(body, mesh.shape["path"], mesh.shape["fsdp"]),
        mesh=mesh,
        in_specs=(tokens, tokens, weights, weights, weights, weights, P()),
        out_specs=(weights,) * 4,
        check_vma=False,
    )
```
